512 devices in a mesh: tx: 4 (over y), ty: 8 (over x, core), depth: 16 (over z).
Axes of the slice: x: 4, y: 4, z: 16, core: 2. Of those that a mesh axis runs over, the one named last changes fastest.
Arguments:
- volume: bfloat16 [512, 2048, 512], P('depth', 'ty', 'tx'), may hold values from -6 to 6
- transfer: float32 [4, 2], replicated, may hold values from -1.5 to 1.5
- ray_start: int32 [16, 2048, 512], P('depth', 'ty', 'tx'), may hold values from 0 to 15
- ray_stop: int32 [16, 2048, 512], P('depth', 'ty', 'tx'), may hold values from 16 to 32
- pattern: int32 [16, 256, 4], P('depth', 'ty', 'tx'), may hold values 0 or 1
- depth_order: int32 [16], replicated, may hold values from 0 to 15, each once
Outputs:
- frame: float32 [4, 2048, 512], P(None, 'ty', 'tx')
The draws below stay inside these ranges and needn't reach their ends.
Inputs may be any that keep to these rules, and one draw needn't show every extreme that they name: ray_start[s] < ray_stop[s] for every ray and slice. `depth_order`: each slice appears once.
All inputs are finite; a program needn't handle non-finite values. No bound on the sum of `pattern` on one device may be relied on, other than what follows from the above.
Results may differ from the reference program's by a relative error of at most 0.0003.
Values may be sent and summed in bfloat16 or wider, within the bound.
No kernel may reach another device: no remote copies, remote signals or barrier semaphores. Data moves between devices by JAX's collectives and lax.ppermute only.
A program may use at most 64 MiB of HBM per device.

```python
import jax
import jax.numpy as jnp
from jax import lax

BZ = 32
NZ = 512
NY = 2048
NX = 512
N_DEPTH = 16


def set_ends(result, key, least, top_value):
    spot = [jax.random.randint(jax.random.fold_in(key, axis), (), 0, length) for axis, length in enumerate(result.shape)]
    widest = result.shape.index(max(result.shape))
    neighbour = spot[:widest] + [(spot[widest] + 1) % result.shape[widest]] + spot[widest + 1:]
    return result.at[tuple(spot)].set(least).at[tuple(neighbour)].set(top_value)


def shard_levels(stream_key, shape, split, smallest, largest):
    loudness = 1.0
    for dim, shards_of in split:
        steps = jax.random.uniform(jax.random.fold_in(jax.random.fold_in(stream_key, 6), dim), (shards_of,), jnp.float32, smallest / len(split), largest / len(split))
        loudness = loudness * jnp.repeat(jnp.exp(steps), shape[dim] // shards_of).reshape((-1,) + (1,) * (len(shape) - 1 - dim))
    return loudness


def scatter_about(key, shape, scale, reach, split=(), kind=jnp.bfloat16):
    loudness = shard_levels(key, shape, split, -0.22, 0.18) if split else 1.0
    values = jax.random.normal(key, shape, jnp.float32) * scale * loudness
    return jnp.minimum(jnp.maximum(values, -reach), reach).astype(kind)


def setup_inputs(seed: int = 0) -> dict:
    splits = jax.random.split(jax.random.key(seed), 7)
    return {
        "volume": scatter_about(splits[0], (NZ, NY, NX), 1.0, 6.0, ((0, 16), (1, 8), (2, 4))),
        "transfer": jnp.clip(jax.random.uniform(splits[1], (4, 2), jnp.float32, -1.5, 1.5), -1.5, 1.5),
        "ray_start": set_ends(jax.random.randint(splits[2], (N_DEPTH, NY, NX), 0, BZ // 2), jax.random.fold_in(splits[2], 1), 0, (BZ // 2) - 1).astype(jnp.int32),
        "ray_stop": set_ends(jax.random.randint(splits[3], (N_DEPTH, NY, NX), BZ // 2, BZ + 1), jax.random.fold_in(splits[3], 1), BZ // 2, BZ).astype(jnp.int32),
        "pattern": set_ends((jax.random.randint(splits[4], (N_DEPTH, NY // 8, NX // 128), 0, 4) < 3).astype(jnp.int32), jax.random.fold_in(splits[4], 1), 0, 1),
        "depth_order": jax.random.permutation(splits[5], N_DEPTH).astype(jnp.int32),
    }


def local_partial(padded, transfer, ray_start, ray_stop, pattern, depth_count):
    samples = padded.shape[0] - 2
    values = padded[1:-1, 1:-1, 1:-1]
    grad_z = (padded[2:, 1:-1, 1:-1] - padded[:-2, 1:-1, 1:-1]) * 0.5
    grad_y = (padded[1:-1, 2:, 1:-1] - padded[1:-1, :-2, 1:-1]) * 0.5
    grad_x = (padded[1:-1, 1:-1, 2:] - padded[1:-1, 1:-1, :-2]) * 0.5
    lit = jnp.abs(0.48 * grad_x + 0.6 * grad_y + 0.64 * grad_z)
    shading = 0.3 + 0.7 * lit / jnp.sqrt(grad_x * grad_x + grad_y * grad_y + grad_z * grad_z + 1.0)
    rows_each = ray_start.shape[0] // pattern.shape[0]
    cols_each = ray_start.shape[1] // pattern.shape[1]
    pattern_full = jnp.repeat(jnp.repeat(pattern, rows_each, axis=0), cols_each, axis=1)
    layers = lax.broadcasted_iota(jnp.int32, (samples, 1, 1), 0)
    active = (layers >= ray_start[None]) & (layers < ray_stop[None]) & (pattern_full[None] > 0)
    density = jax.nn.softplus(transfer[3, 0] * values + transfer[3, 1]) * (2.0 / (samples * depth_count))
    opacity = jnp.where(active, 1.0 - jnp.exp(-density), jnp.float32(0.0))
    passed = jnp.cumprod(1.0 - opacity, axis=0)
    prior = jnp.concatenate([jnp.ones_like(passed[:1]), passed[:-1]], axis=0)
    weights = prior * opacity * shading
    tinted = jax.nn.sigmoid(transfer[:3, 0][:, None, None, None] * values[None] + transfer[:3, 1][:, None, None, None])
    colors = lax.optimization_barrier(jnp.sum(weights[None] * tinted, axis=1))
    return jnp.concatenate([colors, passed[-1][None]], axis=0)

def composite(partials, depth_order):
    count = partials.shape[0]

    def step(position, state_pair):
        colors, remain = state_pair
        slice_part = lax.dynamic_index_in_dim(partials, depth_order[position], 0, keepdims=False)
        return (colors + remain[None] * slice_part[:3], remain * slice_part[3])
    start_pair = (jnp.zeros(partials.shape[1:2 - 1 + 1][:0] + (3,) + partials.shape[2:], jnp.float32), jnp.ones(partials.shape[2:], jnp.float32))
    colors, remain = lax.fori_loop(0, count, step, start_pair)
    return jnp.concatenate([colors, 1.0 - remain[None]], axis=0)

def reference(volume, transfer, ray_start, ray_stop, pattern, depth_order):
    padz = jnp.pad(volume, ((1, 1), (0, 0), (0, 0)))

    def one_slice(slice_index):
        bricks = lax.dynamic_slice_in_dim(padz, slice_index * BZ, BZ + 2, 0).astype(jnp.float32)
        bricks = jnp.pad(bricks, ((0, 0), (1, 1), (1, 1)))
        return local_partial(bricks, transfer, ray_start[slice_index], ray_stop[slice_index], pattern[slice_index], N_DEPTH)
    partials = lax.map(one_slice, jnp.arange(N_DEPTH, dtype=jnp.int32))
    return composite(partials, depth_order)
```

```python
import jax
import jax.numpy as jnp
from jax import lax
from jax.experimental import pallas as pl
from jax.experimental.pallas import tpu as pltpu
from jax.sharding import PartitionSpec as P

LOG2E = 1.4426950408889634
CODE = 65535.0
VMEM = pltpu.VMEM
SMEM = pltpu.SMEM


def iota(shape, dim):
    return lax.broadcasted_iota(jnp.int32, shape, dim)


def encode(low, high):
    def code(x):
        root = jnp.sqrt(jnp.sqrt(jnp.maximum(x, 0.0)))
        return jnp.minimum(root * CODE + 0.5, CODE).astype(jnp.int32)

    return code(low) | (code(high) << 16)


def decode(word):
    def value(c):
        square = (c.astype(jnp.float32) * (1.0 / CODE)) ** 2
        return square * square

    return value(word & 0xFFFF), value(lax.shift_right_logical(word, 16))


def edges_kernel(vol, z0, z1, y0, y1, xt):
    layers, rows, cols = vol.shape
    z0[...] = vol[0]
    z1[...] = vol[layers - 1]
    y0[...] = vol[:, 0:16, :][:, 0, :]
    y1[...] = vol[:, rows - 16 : rows, :][:, 15, :]
    r, c = (iota((2 * cols, cols), 0), iota((2 * cols, cols), 1))
    total = jnp.zeros((rows, cols), jnp.float32)
    for k in range(0, layers, 2):
        pick = ((r % cols == 0) & (c - r // cols == k)) | (
            (r % cols == cols - 1) & (c - r // cols == k + layers)
        )
        pair = jnp.concatenate([vol[k], vol[k + 1]], axis=1)
        total = total + jnp.dot(
            pair, pick.astype(jnp.float32).astype(jnp.bfloat16), preferred_element_type=jnp.float32
        )
    xt[...] = total.astype(jnp.bfloat16)


def render_kernel(
    tf, pat, vol, zlo, zhi, ylo, yhi, xlo, xhi, start, stop, out, sx_all, sy_all, count, step_rows
):
    layers, rows, cols = vol.shape
    f32, bf16 = (jnp.float32, jnp.bfloat16)

    lane = iota((rows, cols), 1)
    side = jnp.where(lane < layers, xhi[...].astype(f32), xlo[...].astype(f32)).astype(bf16)
    r, c = (iota((cols, cols), 0), iota((cols, cols), 1))
    dx = ((r == c + 1).astype(f32) - (r == c - 1).astype(f32)).astype(bf16)
    yr, yc = (iota((rows, rows), 0), iota((rows, rows), 1))
    dy = ((yc == yr + 1).astype(f32) - (yc == yr - 1).astype(f32)).astype(bf16)
    at_low, at_high = (jnp.where(c == 0, r, -1), jnp.where(c == cols - 1, r, -1))

    def gradients(k, carry):
        v = vol[k]
        ends = ((at_high == k).astype(f32) - (at_low == k + layers).astype(f32)).astype(bf16)
        sx_all[k] = jnp.dot(
            jnp.concatenate([v, side], axis=1),
            jnp.concatenate([dx, ends], axis=0),
            preferred_element_type=f32,
        )
        sy_all[k] = jnp.dot(dy, v, preferred_element_type=f32)
        return carry

    lax.fori_loop(0, layers, gradients, 0, unroll=2)
    sub = iota((layers, 8, cols), 1)
    sy_all[:, 0:8, :] = sy_all[:, 0:8, :] - jnp.where(sub == 0, ylo[...].astype(f32)[:, None, :], 0.0)
    sy_all[:, rows - 8 : rows, :] = sy_all[:, rows - 8 : rows, :] + jnp.where(
        sub == 7, yhi[...].astype(f32)[:, None, :], 0.0
    )

    slopes = [tf[j, 0] * 0.5 for j in range(3)]
    offsets = [tf[j, 1] * 0.5 for j in range(3)]
    dens_slope, dens_offset = (tf[3, 0] * LOG2E, tf[3, 1] * LOG2E)
    scale = -LOG2E * 2.0 / (layers * count)

    def chunk(i, carry):
        base = pl.multiple_of(i * step_rows, step_rows)
        here = pl.ds(base, step_rows)
        group = iota((step_rows, cols), 0) // 8
        begin, end = (start[here, :], stop[here, :])
        on = jnp.zeros((step_rows, cols), jnp.int32)
        for g in range(step_rows // 8):
            on = jnp.where(group == g, pat[i * (step_rows // 8) + g], on)
        end = jnp.where(on > 0, end, 0)
        zero = jnp.zeros((step_rows, cols), f32)
        depth, before, shaded = (zero, zero + 1.0, zero)
        tints = [zero, zero, zero]
        below, value = (zlo[here, :].astype(f32), vol[0, here, :].astype(f32))
        for k in range(layers):
            above = (vol[k + 1, here, :] if k + 1 < layers else zhi[here, :]).astype(f32)
            sx, sy, sz = (sx_all[k, here, :], sy_all[k, here, :], above - below)
            lit = jnp.abs((0.48 * 0.7) * sx + (0.6 * 0.7) * sy + (0.64 * 0.7) * sz)
            shading = 0.3 + lit * lax.rsqrt(sx * sx + sy * sy + sz * sz + 4.0)
            soft = jnp.log(1.0 + jnp.exp2(dens_slope * value + dens_offset))
            active = (begin <= k) & (end > k)
            depth = depth + jnp.where(active, soft, 0.0)
            after = jnp.exp2(depth * scale)
            weight = (before - after) * shading
            shaded = shaded + weight
            tints = [
                t + weight * jnp.tanh(s * value + o) for t, s, o in zip(tints, slopes, offsets)
            ]
            below, value, before = (value, above, after)
        red, green, blue = [0.5 * (shaded + t) for t in tints]
        first, second = (encode(red, green), encode(blue, 1.0 - before))
        share = rows // count
        for j in range(step_rows // share):
            out[i * (step_rows // share) + j, 0] = first[j * share : (j + 1) * share]
            out[i * (step_rows // share) + j, 1] = second[j * share : (j + 1) * share]
        return carry

    lax.fori_loop(0, rows // step_rows, chunk, 0)


def composite_kernel(order, parts, out):
    count, _, rows, cols = parts.shape

    def step(r, state):
        red, green, blue, left = state
        s = order[r]
        one, two = (decode(parts[s, 0]), decode(parts[s, 1]))
        return (red + left * one[0], green + left * one[1], blue + left * two[0], left * (1.0 - two[1]))

    zero = jnp.zeros((rows, cols), jnp.float32)
    state = (zero, zero, zero, zero + 1.0)
    for r in range(count):
        state = step(r, state)
    red, green, blue, left = state
    first, second = (encode(red, green), encode(blue, 1.0 - left))
    for s in range(count):
        out[s, 0] = first
        out[s, 1] = second


def frame_kernel(words, out):
    count, _, rows, cols = words.shape
    for s in range(count):
        here = slice(s * rows, (s + 1) * rows)
        for w in range(2):
            low, high = decode(words[s, w])
            out[2 * w, here, :] = low
            out[2 * w + 1, here, :] = high


def halo(array, axis, shift):
    count = lax.axis_size(axis)
    pairs = [(i, i + shift) for i in range(count) if 0 <= i + shift < count]
    return lax.ppermute(array, axis, pairs)


def shards(volume, transfer, ray_start, ray_stop, pattern, depth_order):
    layers, rows, cols = volume.shape
    count = lax.axis_size("depth")
    bf16, f32 = (jnp.bfloat16, jnp.float32)
    limit = pltpu.CompilerParams(vmem_limit_bytes=40 * 1024 * 1024)
    vmem = pl.BlockSpec(memory_space=VMEM)
    smem = pl.BlockSpec(memory_space=SMEM)
    shape = jax.ShapeDtypeStruct

    z0, z1, y0, y1, xt = pl.pallas_call(
        edges_kernel,
        out_shape=[
            shape((rows, cols), bf16),
            shape((rows, cols), bf16),
            shape((layers, cols), bf16),
            shape((layers, cols), bf16),
            shape((rows, cols), bf16),
        ],
        in_specs=[vmem],
        out_specs=[vmem] * 5,
        compiler_params=limit,
        name="edges",
    )(volume)
    zlo, zhi = (halo(z1, "depth", 1), halo(z0, "depth", -1))
    ylo, yhi = (halo(y1, "ty", 1), halo(y0, "ty", -1))
    xlo, xhi = (halo(xt, "tx", 1), halo(xt, "tx", -1))

    step_rows = 32
    share = rows // count
    words = pl.pallas_call(
        lambda *refs: render_kernel(*refs, count=count, step_rows=step_rows),
        out_shape=shape((count, 2, share, cols), jnp.int32),
        in_specs=[smem, smem] + [vmem] * 9,
        out_specs=vmem,
        scratch_shapes=[VMEM((layers, rows, cols), f32), VMEM((layers, rows, cols), f32)],
        compiler_params=limit,
        name="render",
    )(transfer, pattern.reshape(-1), volume, zlo, zhi, ylo, yhi, xlo, xhi, ray_start[0], ray_stop[0])

    words = lax.all_to_all(words, "depth", split_axis=0, concat_axis=0, tiled=True)
    words = pl.pallas_call(
        composite_kernel,
        out_shape=shape(words.shape, jnp.int32),
        in_specs=[smem, vmem],
        out_specs=vmem,
        compiler_params=limit,
        name="composite",
    )(depth_order, words)
    words = lax.all_to_all(words, "depth", split_axis=0, concat_axis=0, tiled=True)
    return pl.pallas_call(
        frame_kernel,
        out_shape=shape((4, rows, cols), f32),
        in_specs=[vmem],
        out_specs=vmem,
        compiler_params=limit,
        name="frame",
    )(words)


def solution(mesh):
    in_specs = (
        P("depth", "ty", "tx"),
        P(),
        P("depth", "ty", "tx"),
        P("depth", "ty", "tx"),
        P("depth", "ty", "tx"),
        P(),
    )
    out_specs = P(None, "ty", "tx")
    return jax.shard_map(shards, mesh=mesh, in_specs=in_specs, out_specs=out_specs, check_vma=False)
```

```python
import jax
import jax.numpy as jnp
from jax import lax
from jax.experimental import pallas as pl
from jax.experimental.pallas import tpu as pltpu
from jax.sharding import PartitionSpec as P

LOG2E = 1.4426950408889634
CODE = 65535.0
VMEM = pltpu.VMEM
SMEM = pltpu.SMEM


def iota(shape, dim):
    return lax.broadcasted_iota(jnp.int32, shape, dim)


def encode(low, high):
    def code(x):
        root = jnp.sqrt(jnp.sqrt(jnp.maximum(x, 0.0)))
        return jnp.minimum(root * CODE + 0.5, CODE).astype(jnp.int32)

    return code(low) | (code(high) << 16)


def decode(word):
    def value(c):
        square = (c.astype(jnp.float32) * (1.0 / CODE)) ** 2
        return square * square

    return value(word & 0xFFFF), value(lax.shift_right_logical(word, 16))


def faces_kernel(vol, z0, z1, y0, y1, first, last, sems):
    layers, rows, _ = vol.shape
    copies = [
        pltpu.make_async_copy(vol.at[0], z0, sems.at[0]),
        pltpu.make_async_copy(vol.at[layers - 1], z1, sems.at[1]),
        pltpu.make_async_copy(vol.at[:, pl.ds(0, 16), :], first, sems.at[2]),
        pltpu.make_async_copy(vol.at[:, pl.ds(rows - 16, 16), :], last, sems.at[3]),
    ]
    for copy in copies:
        copy.start()
    for copy in copies:
        copy.wait()
    y0[...] = first[...][:, 0, :]
    y1[...] = last[...][:, 15, :]


def sides_kernel(vol, arrived, xt):
    layers, rows, cols = vol.shape
    r, c = (iota((2 * cols, cols), 0), iota((2 * cols, cols), 1))
    total = jnp.zeros((rows, cols), jnp.float32)
    for k in range(0, layers, 2):
        pick = ((r % cols == 0) & (c - r // cols == k)) | (
            (r % cols == cols - 1) & (c - r // cols == k + layers)
        )
        pair = jnp.concatenate([vol[k], vol[k + 1]], axis=1)
        total = total + jnp.dot(
            pair, pick.astype(jnp.float32).astype(jnp.bfloat16), preferred_element_type=jnp.float32
        )
    xt[...] = total.astype(jnp.bfloat16)


def absorb_kernel(tf, pat, vol, start, stop, weights, alpha, begin, end, sems, count, step_rows):
    layers, rows, cols = vol.shape
    f32 = jnp.float32
    copies = [
        pltpu.make_async_copy(start, begin, sems.at[0]),
        pltpu.make_async_copy(stop, end, sems.at[1]),
    ]
    for copy in copies:
        copy.start()
    for copy in copies:
        copy.wait()
    slope, offset = (tf[3, 0] * LOG2E, tf[3, 1] * LOG2E)
    scale = -LOG2E * 2.0 / (layers * count)
    half = layers // 2

    def chunk(i, carry):
        here = pl.ds(pl.multiple_of(i * step_rows, step_rows), step_rows)
        group = iota((step_rows, cols), 0) // 8
        on = jnp.zeros((step_rows, cols), jnp.int32)
        for g in range(step_rows // 8):
            on = jnp.where(group == g, pat[i * (step_rows // 8) + g], on)
        enter = jnp.where(on > 0, begin[here, :], layers)
        leave = jnp.where(on > 0, end[here, :], 0)
        depth = jnp.zeros((step_rows, cols), f32)
        before = depth + 1.0
        for k in range(layers):
            soft = jnp.log(1.0 + jnp.exp2(slope * vol[k, here, :].astype(f32) + offset))
            active = enter <= k if k < half else leave > k
            depth = depth + jnp.where(active, soft, 0.0)
            after = jnp.exp2(depth * scale)
            weights[k, here, :] = before - after
            before = after
        alpha[here, :] = 1.0 - before
        return carry

    lax.fori_loop(0, rows // step_rows, chunk, 0)


def shade_kernel(
    tf, vol, weights, alpha, zlo, zhi, ylo, yhi, xlo, xhi, out, field, sx_all, count, step_rows
):
    layers, rows, cols = vol.shape
    f32, bf16 = (jnp.float32, jnp.bfloat16)
    lane = iota((rows, cols), 1)
    side = jnp.where(lane < layers, xhi[...].astype(f32), xlo[...].astype(f32))
    r, c = (iota((2 * cols, cols), 0), iota((2 * cols, cols), 1))
    inner = r < cols
    plus = ((r == c + 1) & inner) | ((r >= cols) & (r < cols + layers) & (c == cols - 1))
    minus = ((r == c - 1) & inner) | ((r >= cols + layers) & (r < cols + 2 * layers) & (c == 0))
    delta = (plus.astype(f32) - minus.astype(f32)).astype(bf16)
    phase = jnp.where(lane < 2 * layers, lane % layers, layers)

    sub = iota((layers, 8, cols), 1)
    field[:, 0:8, :] = jnp.where(sub == 7, ylo[...].astype(f32)[:, None, :], 0.0)
    field[:, rows + 8 : rows + 16, :] = jnp.where(sub == 0, yhi[...].astype(f32)[:, None, :], 0.0)

    def along_x(k, carry):
        value = vol[k]
        field[k, 8 : rows + 8, :] = value.astype(f32)
        ends = jnp.where(phase == k, side, 0.0).astype(bf16)
        sx_all[k] = jnp.dot(
            jnp.concatenate([value, ends], axis=1), delta, preferred_element_type=f32
        )
        return carry

    lax.fori_loop(0, layers, along_x, 0, unroll=8)

    slopes = [tf[j, 0] * 0.5 for j in range(3)]
    offsets = [tf[j, 1] * 0.5 for j in range(3)]
    strength = 0.64 * 0.7

    def chunk(i, carry):
        base = pl.multiple_of(i * step_rows, step_rows)
        here = pl.ds(base, step_rows)
        zero = jnp.zeros((step_rows, cols), f32)
        shaded, tints = (zero, [zero, zero, zero])
        middle = pl.ds(pl.multiple_of(base + 8, 8), step_rows)
        below, value = (zlo[here, :].astype(f32), field[0, middle, :])
        for k in range(layers):
            above = field[k + 1, middle, :] if k + 1 < layers else zhi[here, :].astype(f32)
            sx, sz = (sx_all[k, here, :], above - below)
            sy = field[k, pl.ds(base + 9, step_rows), :] - field[k, pl.ds(base + 7, step_rows), :]
            lit = jnp.abs((0.48 / 0.64) * sx + (0.6 / 0.64) * sy + sz)
            bright = lit * lax.rsqrt(sx * sx + sy * sy + sz * sz + 4.0) + 0.3 / strength
            weight = weights[k, here, :] * bright
            shaded = shaded + weight
            tints = [
                t + weight * jnp.tanh(s * value + o) for t, s, o in zip(tints, slopes, offsets)
            ]
            below, value = (value, above)
        red, green, blue = [(0.5 * strength) * (shaded + t) for t in tints]
        first, second = (encode(red, green), encode(blue, alpha[here, :]))
        share = rows // count
        for j in range(step_rows // share):
            out[i * (step_rows // share) + j, 0] = first[j * share : (j + 1) * share]
            out[i * (step_rows // share) + j, 1] = second[j * share : (j + 1) * share]
        return carry

    lax.fori_loop(0, rows // step_rows, chunk, 0)


def composite_kernel(order, parts, out):
    count, _, rows, cols = parts.shape

    def step(r, state):
        red, green, blue, left = state
        s = order[r]
        one, two = (decode(parts[s, 0]), decode(parts[s, 1]))
        return (red + left * one[0], green + left * one[1], blue + left * two[0], left * (1.0 - two[1]))

    zero = jnp.zeros((rows, cols), jnp.float32)
    state = (zero, zero, zero, zero + 1.0)
    for r in range(count):
        state = step(r, state)
    red, green, blue, left = state
    first, second = (encode(red, green), encode(blue, 1.0 - left))
    for s in range(count):
        out[s, 0] = first
        out[s, 1] = second


def frame_kernel(words, out):
    count, _, rows, cols = words.shape
    for s in range(count):
        here = slice(s * rows, (s + 1) * rows)
        for w in range(2):
            low, high = decode(words[s, w])
            out[2 * w, here, :] = low
            out[2 * w + 1, here, :] = high


def halo(array, axis, shift):
    count = lax.axis_size(axis)
    pairs = [(i, i + shift) for i in range(count) if 0 <= i + shift < count]
    return lax.ppermute(array, axis, pairs)


def shards(volume, transfer, ray_start, ray_stop, pattern, depth_order):
    layers, rows, cols = volume.shape
    count = lax.axis_size("depth")
    bf16, f32 = (jnp.bfloat16, jnp.float32)
    limit = pltpu.CompilerParams(vmem_limit_bytes=32 * 1024 * 1024)
    vmem = pl.BlockSpec(memory_space=VMEM)
    smem = pl.BlockSpec(memory_space=SMEM)
    shape = jax.ShapeDtypeStruct

    hbm = pl.BlockSpec(memory_space=pltpu.HBM)
    anywhere = pl.BlockSpec(memory_space=pl.ANY)

    z0, z1, y0, y1 = pl.pallas_call(
        faces_kernel,
        out_shape=[shape((rows, cols), bf16)] * 2 + [shape((layers, cols), bf16)] * 2,
        in_specs=[hbm],
        out_specs=[vmem] * 4,
        scratch_shapes=[VMEM((layers, 16, cols), bf16)] * 2 + [pltpu.SemaphoreType.DMA((4,))],
        compiler_params=limit,
        name="faces",
    )(volume)
    zlo, zhi = (halo(z1, "depth", 1), halo(z0, "depth", -1))
    ylo, yhi = (halo(y1, "ty", 1), halo(y0, "ty", -1))
    xt = pl.pallas_call(
        sides_kernel,
        out_shape=shape((rows, cols), bf16),
        in_specs=[vmem, anywhere],
        out_specs=vmem,
        compiler_params=limit,
        name="sides",
    )(volume, zlo)
    xlo, xhi = (halo(xt, "tx", 1), halo(xt, "tx", -1))

    step_rows = 32
    share = rows // count
    weights, alpha = pl.pallas_call(
        lambda *refs: absorb_kernel(*refs, count=count, step_rows=step_rows),
        out_shape=[shape((layers, rows, cols), f32), shape((rows, cols), f32)],
        in_specs=[smem, smem, vmem, hbm, hbm],
        out_specs=[vmem] * 2,
        scratch_shapes=[VMEM((rows, cols), jnp.int32)] * 2 + [pltpu.SemaphoreType.DMA((2,))],
        compiler_params=limit,
        cost_estimate=pl.CostEstimate(
            flops=12 * volume.size, bytes_accessed=6 * volume.size, transcendentals=3 * volume.size
        ),
        name="absorb",
    )(transfer, pattern.reshape(-1), volume, ray_start[0], ray_stop[0])
    words = pl.pallas_call(
        lambda *refs: shade_kernel(*refs, count=count, step_rows=step_rows),
        out_shape=shape((count, 2, share, cols), jnp.int32),
        in_specs=[smem] + [vmem] * 9,
        out_specs=vmem,
        scratch_shapes=[VMEM((layers, rows + 16, cols), f32), VMEM((layers, rows, cols), f32)],
        compiler_params=limit,
        cost_estimate=pl.CostEstimate(
            flops=40 * volume.size, bytes_accessed=6 * volume.size, transcendentals=4 * volume.size
        ),
        name="shade",
    )(transfer, volume, weights, alpha, zlo, zhi, ylo, yhi, xlo, xhi)

    words = lax.all_to_all(words, "depth", split_axis=0, concat_axis=0, tiled=True)
    words = pl.pallas_call(
        composite_kernel,
        out_shape=shape(words.shape, jnp.int32),
        in_specs=[smem, vmem],
        out_specs=vmem,
        compiler_params=limit,
        name="composite",
    )(depth_order, words)
    words = lax.all_to_all(words, "depth", split_axis=0, concat_axis=0, tiled=True)
    return pl.pallas_call(
        frame_kernel,
        out_shape=shape((4, rows, cols), f32),
        in_specs=[vmem],
        out_specs=vmem,
        compiler_params=limit,
        name="frame",
    )(words)


def solution(mesh):
    in_specs = (
        P("depth", "ty", "tx"),
        P(),
        P("depth", "ty", "tx"),
        P("depth", "ty", "tx"),
        P("depth", "ty", "tx"),
        P(),
    )
    out_specs = P(None, "ty", "tx")
    return jax.shard_map(shards, mesh=mesh, in_specs=in_specs, out_specs=out_specs, check_vma=False)
```

```python
import jax
import jax.numpy as jnp
from jax import lax
from jax.experimental import pallas as pl
from jax.experimental.pallas import tpu as pltpu
from jax.sharding import PartitionSpec as P

LOG2E = 1.4426950408889634
CODE = 65535.0
PARTS = 2
VMEM = pltpu.VMEM
SMEM = pltpu.SMEM


def iota(shape, dim):
    return lax.broadcasted_iota(jnp.int32, shape, dim)


def encode(low, high):
    def code(x):
        root = jnp.sqrt(jnp.sqrt(jnp.maximum(x, 0.0)))
        return jnp.minimum(root * CODE + 0.5, CODE).astype(jnp.int32)

    return code(low) | (code(high) << 16)


def decode(word):
    def value(c):
        square = (c.astype(jnp.float32) * (1.0 / CODE)) ** 2
        return square * square

    return value(word & 0xFFFF), value(lax.shift_right_logical(word, 16))


def open_kernel(volume, start, stop, z0, z1, xt, field, begin, end, vol, sems):
    layers, rows, cols = vol.shape
    parts = sems.shape[0] - 2
    each = layers // parts
    copies = [
        pltpu.make_async_copy(
            volume.at[pl.ds(p * each, each)], vol.at[pl.ds(p * each, each)], sems.at[p]
        )
        for p in range(parts)
    ]
    copies.append(pltpu.make_async_copy(start, begin, sems.at[parts]))
    copies.append(pltpu.make_async_copy(stop, end, sems.at[parts + 1]))
    for copy in copies:
        copy.start()
    r, c = (iota((2 * cols, cols), 0), iota((2 * cols, cols), 1))
    column, second = (r % cols, r // cols)
    total = jnp.zeros((rows, cols), jnp.float32)
    for k in range(0, layers, 2):
        if k % each == 0:
            copies[k // each].wait()
        lane = 2 * (k + second)
        pick = ((column == 0) & (c == lane)) | ((column == cols - 1) & (c == (lane + cols - 1) % cols))
        one, two = (vol[k], vol[k + 1])
        field[k, 8 : rows + 8, :] = one.astype(jnp.float32)
        field[k + 1, 8 : rows + 8, :] = two.astype(jnp.float32)
        total = total + jnp.dot(
            jnp.concatenate([one, two], axis=1),
            pick.astype(jnp.float32).astype(jnp.bfloat16),
            preferred_element_type=jnp.float32,
        )
    z0[...] = vol[0]
    z1[...] = vol[layers - 1]
    xt[...] = total.astype(jnp.bfloat16)
    for copy in copies[parts:]:
        copy.wait()


def rows_kernel(field, arrived, y0, y1):
    rows = field.shape[1] - 16
    y0[...] = field[:, 8:16, :][:, 0, :].astype(jnp.bfloat16)
    y1[...] = field[:, rows : rows + 8, :][:, 7, :].astype(jnp.bfloat16)


def absorb_kernel(tf, pat, field, begin, end, weights, alpha, *, count, step_rows):
    layers, rows, cols = weights.shape
    f32 = jnp.float32
    slope, offset = (tf[0, 3] * LOG2E, tf[1, 3] * LOG2E)
    scale = -LOG2E * 2.0 / (layers * count)
    half = layers // 2

    def chunk(i, carry):
        base = pl.multiple_of(i * step_rows, step_rows)
        here = pl.ds(base, step_rows)
        middle = pl.ds(pl.multiple_of(base + 8, 8), step_rows)
        group = iota((step_rows, cols), 0) // 8
        on = jnp.zeros((step_rows, cols), jnp.int32)
        for g in range(step_rows // 8):
            on = jnp.where(group == g, pat[i * (step_rows // 8) + g], on)
        enter = jnp.where(on > 0, begin[here, :], layers)
        leave = jnp.where(on > 0, end[here, :], 0)
        depth = jnp.zeros((step_rows, cols), f32)
        before = depth + 1.0
        for k in range(layers):
            soft = jnp.log(1.0 + jnp.exp2(slope * field[k, middle, :] + offset))
            active = enter <= k if k < half else leave > k
            depth = depth + jnp.where(active, soft, 0.0)
            after = jnp.exp2(depth * scale)
            weights[k, here, :] = before - after
            before = after
        alpha[here, :] = 1.0 - before
        return carry

    lax.fori_loop(0, rows // step_rows, chunk, 0)


def shade_kernel(
    tf, middle_rows, weights, alpha, zlo, zhi, ylo, yhi, xlo, xhi, out, field, ends, *, count, step_rows
):
    del middle_rows
    layers, rows, cols = weights.shape
    f32 = jnp.float32
    sub = iota((layers, 8, cols), 1)
    field[:, 0:8, :] = jnp.where(sub == 7, ylo[...].astype(f32)[:, None, :], 0.0)
    field[:, rows + 8 : rows + 16, :] = jnp.where(sub == 0, yhi[...].astype(f32)[:, None, :], 0.0)

    slopes = [tf[0, j] * 0.5 for j in range(3)]
    offsets = [tf[1, j] * 0.5 for j in range(3)]
    strength = 0.64 * 0.7
    lane = iota((step_rows, cols), 1)
    first_lane, last_lane = (lane == 0, lane == cols - 1)

    def chunk(i, carry):
        base = pl.multiple_of(i * step_rows, step_rows)
        here = pl.ds(base, step_rows)
        middle = pl.ds(pl.multiple_of(base + 8, 8), step_rows)
        sides = jnp.where(lane % 2 == 0, xhi[here, :].astype(f32), xlo[here, :].astype(f32))
        for k in range(layers):
            ends[k] = sides if k == 0 else pltpu.roll(sides, cols - 2 * k, 1)
        zero = jnp.zeros((step_rows, cols), f32)
        shaded, tints = (zero, [zero, zero, zero])
        below, value = (zlo[here, :].astype(f32), field[0, middle, :])
        for k in range(layers):
            above = field[k + 1, middle, :] if k + 1 < layers else zhi[here, :].astype(f32)
            right = pltpu.roll(jnp.where(first_lane, ends[k], value), cols - 1, 1)
            left = pltpu.roll(jnp.where(last_lane, ends[k], value), 1, 1)
            sx, sz = (right - left, above - below)
            sy = field[k, pl.ds(base + 9, step_rows), :] - field[k, pl.ds(base + 7, step_rows), :]
            lit = jnp.abs((0.48 / 0.64) * sx + (0.6 / 0.64) * sy + sz)
            bright = lit * lax.rsqrt(sx * sx + sy * sy + sz * sz + 4.0) + 0.3 / strength
            weight = weights[k, here, :] * bright
            shaded = shaded + weight
            tints = [
                t + weight * jnp.tanh(s * value + o) for t, s, o in zip(tints, slopes, offsets)
            ]
            below, value = (value, above)
        red, green, blue = [(0.5 * strength) * (shaded + t) for t in tints]
        first, second = (encode(red, green), encode(blue, alpha[here, :]))
        share = rows // count
        for j in range(step_rows // share):
            out[i * (step_rows // share) + j, 0] = first[j * share : (j + 1) * share]
            out[i * (step_rows // share) + j, 1] = second[j * share : (j + 1) * share]
        return carry

    lax.fori_loop(0, rows // step_rows, chunk, 0)


def composite_kernel(order, parts, out):
    count, _, rows, cols = parts.shape

    def step(r, state):
        red, green, blue, left = state
        s = order[r]
        one, two = (decode(parts[s, 0]), decode(parts[s, 1]))
        return (red + left * one[0], green + left * one[1], blue + left * two[0], left * (1.0 - two[1]))

    zero = jnp.zeros((rows, cols), jnp.float32)
    state = (zero, zero, zero, zero + 1.0)
    for r in range(count):
        state = step(r, state)
    red, green, blue, left = state
    first, second = (encode(red, green), encode(blue, 1.0 - left))
    for s in range(count):
        out[s, 0] = first
        out[s, 1] = second


def frame_kernel(words, out):
    count, _, rows, cols = words.shape
    for s in range(count):
        here = slice(s * rows, (s + 1) * rows)
        for w in range(2):
            low, high = decode(words[s, w])
            out[2 * w, here, :] = low
            out[2 * w + 1, here, :] = high


def halo(array, axis, shift):
    count = lax.axis_size(axis)
    pairs = [(i, i + shift) for i in range(count) if 0 <= i + shift < count]
    return lax.ppermute(array, axis, pairs)


def shards(volume, transfer, ray_start, ray_stop, pattern, depth_order):
    layers, rows, cols = volume.shape
    count = lax.axis_size("depth")
    bf16, f32 = (jnp.bfloat16, jnp.float32)
    limit = pltpu.CompilerParams(vmem_limit_bytes=20 * 1024 * 1024)
    vmem = pl.BlockSpec(memory_space=VMEM)
    smem = pl.BlockSpec(memory_space=SMEM)
    shape = jax.ShapeDtypeStruct

    hbm = pl.BlockSpec(memory_space=pltpu.HBM)
    anywhere = pl.BlockSpec(memory_space=pl.ANY)

    whole = shape((rows, cols), bf16)
    bounds = shape((rows, cols), jnp.int32)
    z0, z1, xt, field, begin, end = pl.pallas_call(
        open_kernel,
        out_shape=[whole] * 3 + [shape((layers, rows + 16, cols), f32)] + [bounds] * 2,
        in_specs=[hbm] * 3,
        out_specs=[vmem] * 6,
        scratch_shapes=[VMEM(volume.shape, bf16), pltpu.SemaphoreType.DMA((PARTS + 2,))],
        compiler_params=limit,
        name="open",
    )(*[pltpu.with_memory_space_constraint(x, pltpu.HBM) for x in (volume, ray_start[0], ray_stop[0])])
    zlo, zhi = (halo(z1, "depth", 1), halo(z0, "depth", -1))
    xlo, xhi = (halo(xt, "tx", 1), halo(xt, "tx", -1))
    y0, y1 = pl.pallas_call(
        rows_kernel,
        out_shape=[shape((layers, cols), bf16)] * 2,
        in_specs=[vmem, anywhere],
        out_specs=[vmem] * 2,
        compiler_params=limit,
        name="rows",
    )(field, zlo)
    ylo, yhi = (halo(y1, "ty", 1), halo(y0, "ty", -1))

    step_rows = 32
    share = rows // count
    slopes = transfer.T
    weights, alpha = pl.pallas_call(
        lambda *refs: absorb_kernel(*refs, count=count, step_rows=step_rows),
        out_shape=[shape((layers, rows, cols), f32), shape((rows, cols), f32)],
        in_specs=[smem, smem] + [vmem] * 3,
        out_specs=[vmem] * 2,
        compiler_params=limit,
        cost_estimate=pl.CostEstimate(
            flops=12 * volume.size, bytes_accessed=8 * volume.size, transcendentals=3 * volume.size
        ),
        name="absorb",
    )(slopes, pattern.reshape(-1), field, begin, end)
    words, _ = pl.pallas_call(
        lambda *refs: shade_kernel(*refs, count=count, step_rows=step_rows),
        out_shape=[shape((count, 2, share, cols), jnp.int32), shape(field.shape, f32)],
        in_specs=[smem] + [vmem] * 9,
        out_specs=[vmem] * 2,
        scratch_shapes=[VMEM((layers, step_rows, cols), f32)],
        input_output_aliases={1: 1},
        compiler_params=limit,
        cost_estimate=pl.CostEstimate(
            flops=40 * volume.size, bytes_accessed=8 * volume.size, transcendentals=4 * volume.size
        ),
        name="shade",
    )(slopes, field, weights, alpha, zlo, zhi, ylo, yhi, xlo, xhi)

    words = lax.all_to_all(words, "depth", split_axis=0, concat_axis=0, tiled=True)
    words = pl.pallas_call(
        composite_kernel,
        out_shape=shape(words.shape, jnp.int32),
        in_specs=[smem, vmem],
        out_specs=vmem,
        compiler_params=limit,
        name="composite",
    )(depth_order, words)
    words = lax.all_to_all(words, "depth", split_axis=0, concat_axis=0, tiled=True)
    return pl.pallas_call(
        frame_kernel,
        out_shape=shape((4, rows, cols), f32),
        in_specs=[vmem],
        out_specs=vmem,
        compiler_params=limit,
        name="frame",
    )(words)


def solution(mesh):
    in_specs = (
        P("depth", "ty", "tx"),
        P(),
        P("depth", "ty", "tx"),
        P("depth", "ty", "tx"),
        P("depth", "ty", "tx"),
        P(),
    )
    out_specs = P(None, "ty", "tx")
    return jax.shard_map(shards, mesh=mesh, in_specs=in_specs, out_specs=out_specs, check_vma=False)
```

```python
import jax
import jax.numpy as jnp
from jax import lax
from jax.experimental import pallas as pl
from jax.experimental.pallas import tpu as pltpu
from jax.sharding import PartitionSpec as P

LOG2E = 1.4426950408889634
CODE = 65535.0
PARTS = 2
VMEM = pltpu.VMEM
SMEM = pltpu.SMEM


def iota(shape, dim):
    return lax.broadcasted_iota(jnp.int32, shape, dim)


def encode(low, high):
    def code(x):
        root = jnp.sqrt(jnp.sqrt(jnp.maximum(x, 0.0)))
        return jnp.minimum(root * CODE + 0.5, CODE).astype(jnp.int32)

    return code(low) | (code(high) << 16)


def decode(word):
    def value(c):
        square = (c.astype(jnp.float32) * (1.0 / CODE)) ** 2
        return square * square

    return value(word & 0xFFFF), value(lax.shift_right_logical(word, 16))


def open_kernel(volume, start, stop, z0, z1, xt, field, begin, end, near, vol, sems):
    layers, rows, cols = vol.shape
    parts = sems.shape[0] - 2
    each = layers // parts
    copies = [
        pltpu.make_async_copy(
            volume.at[pl.ds(p * each, each)], vol.at[pl.ds(p * each, each)], sems.at[p]
        )
        for p in range(parts)
    ]
    copies.append(pltpu.make_async_copy(start, begin, sems.at[parts]))
    copies.append(pltpu.make_async_copy(stop, end, sems.at[parts + 1]))
    for copy in copies:
        copy.start()
    near[...] = neighbours()
    r, c = (iota((2 * cols, cols), 0), iota((2 * cols, cols), 1))
    column, second = (r % cols, r // cols)
    total = jnp.zeros((rows, cols), jnp.float32)
    for k in range(0, layers, 2):
        if k % each == 0:
            copies[k // each].wait()
        lane = 2 * (k + second)
        pick = ((column == 0) & (c == lane)) | ((column == cols - 1) & (c == (lane + cols - 1) % cols))
        one, two = (vol[k], vol[k + 1])
        field[k, 8 : rows + 8, :] = one.astype(jnp.float32)
        field[k + 1, 8 : rows + 8, :] = two.astype(jnp.float32)
        total = total + jnp.dot(
            jnp.concatenate([one, two], axis=1),
            pick.astype(jnp.float32).astype(jnp.bfloat16),
            preferred_element_type=jnp.float32,
        )
    z0[...] = vol[0]
    z1[...] = vol[layers - 1]
    xt[...] = total.astype(jnp.bfloat16)
    for copy in copies[parts:]:
        copy.wait()


def rows_kernel(field, arrived, y0, y1):
    rows = field.shape[1] - 16
    y0[...] = field[:, 8:16, :][:, 0, :].astype(jnp.bfloat16)
    y1[...] = field[:, rows : rows + 8, :][:, 7, :].astype(jnp.bfloat16)


def absorb_kernel(tf, pat, field, begin, end, weights, alpha, *, count, step_rows):
    layers, rows, cols = weights.shape
    f32 = jnp.float32
    slope, offset = (tf[0, 3] * LOG2E, tf[1, 3] * LOG2E)
    scale = -LOG2E * 2.0 / (layers * count)
    half = layers // 2

    def chunk(i, carry):
        base = pl.multiple_of(i * step_rows, step_rows)
        here = pl.ds(base, step_rows)
        middle = pl.ds(pl.multiple_of(base + 8, 8), step_rows)
        group = iota((step_rows, cols), 0) // 8
        on = jnp.zeros((step_rows, cols), jnp.int32)
        for g in range(step_rows // 8):
            on = jnp.where(group == g, pat[i * (step_rows // 8) + g], on)
        enter = jnp.where(on > 0, begin[here, :], layers)
        leave = jnp.where(on > 0, end[here, :], 0)
        depth = jnp.zeros((step_rows, cols), f32)
        before = depth + 1.0
        for k in range(layers):
            soft = jnp.log(1.0 + jnp.exp2(slope * field[k, middle, :] + offset))
            active = enter <= k if k < half else leave > k
            depth = depth + jnp.where(active, soft, 0.0)
            after = jnp.exp2(depth * scale)
            weights[k, here, :] = before - after
            before = after
        alpha[here, :] = 1.0 - before
        return carry

    lax.fori_loop(0, rows // step_rows, chunk, 0)


def shade_kernel(
    tf, middle_rows, weights, alpha, near, zlo, zhi, ylo, yhi, xlo, xhi, out, field, ends,
    *, count, step_rows
):
    del middle_rows
    layers, rows, cols = weights.shape
    f32 = jnp.float32
    sub = iota((layers, 8, cols), 1)
    kept = {axis: (near[2 * i : 2 * i + 1, :], near[2 * i + 1 : 2 * i + 2, :]) for i, axis in enumerate(AXES)}
    low, high = kept["ty"]
    field[:, 0:8, :] = jnp.where(sub == 7, (ylo[...].astype(f32) * low)[:, None, :], 0.0)
    field[:, rows + 8 : rows + 16, :] = jnp.where(
        sub == 0, (yhi[...].astype(f32) * high)[:, None, :], 0.0
    )

    slopes = [tf[0, j] * 0.5 for j in range(3)]
    offsets = [tf[1, j] * 0.5 for j in range(3)]
    strength = 0.64 * 0.7
    lane = iota((step_rows, cols), 1)
    first_lane, last_lane = (lane == 0, lane == cols - 1)

    def chunk(i, carry):
        base = pl.multiple_of(i * step_rows, step_rows)
        here = pl.ds(base, step_rows)
        middle = pl.ds(pl.multiple_of(base + 8, 8), step_rows)
        low, high = kept["tx"]
        sides = jnp.where(
            lane % 2 == 0, xhi[here, :].astype(f32) * high, xlo[here, :].astype(f32) * low
        )
        for k in range(layers):
            ends[k] = sides if k == 0 else pltpu.roll(sides, cols - 2 * k, 1)
        zero = jnp.zeros((step_rows, cols), f32)
        shaded, tints = (zero, [zero, zero, zero])
        low, high = kept["depth"]
        below, value = (zlo[here, :].astype(f32) * low, field[0, middle, :])
        for k in range(layers):
            above = field[k + 1, middle, :] if k + 1 < layers else zhi[here, :].astype(f32) * high
            right = pltpu.roll(jnp.where(first_lane, ends[k], value), cols - 1, 1)
            left = pltpu.roll(jnp.where(last_lane, ends[k], value), 1, 1)
            sx, sz = (right - left, above - below)
            sy = field[k, pl.ds(base + 9, step_rows), :] - field[k, pl.ds(base + 7, step_rows), :]
            lit = jnp.abs((0.48 / 0.64) * sx + (0.6 / 0.64) * sy + sz)
            bright = lit * lax.rsqrt(sx * sx + sy * sy + sz * sz + 4.0) + 0.3 / strength
            weight = weights[k, here, :] * bright
            shaded = shaded + weight
            tints = [
                t + weight * jnp.tanh(s * value + o) for t, s, o in zip(tints, slopes, offsets)
            ]
            below, value = (value, above)
        red, green, blue = [(0.5 * strength) * (shaded + t) for t in tints]
        first, second = (encode(red, green), encode(blue, alpha[here, :]))
        share = rows // count
        for j in range(step_rows // share):
            out[i * (step_rows // share) + j, 0] = first[j * share : (j + 1) * share]
            out[i * (step_rows // share) + j, 1] = second[j * share : (j + 1) * share]
        return carry

    lax.fori_loop(0, rows // step_rows, chunk, 0)


def composite_kernel(order, parts, out):
    count, _, rows, cols = parts.shape

    def step(r, state):
        red, green, blue, left = state
        s = order[r]
        one, two = (decode(parts[s, 0]), decode(parts[s, 1]))
        return (red + left * one[0], green + left * one[1], blue + left * two[0], left * (1.0 - two[1]))

    zero = jnp.zeros((rows, cols), jnp.float32)
    state = (zero, zero, zero, zero + 1.0)
    for r in range(count):
        state = step(r, state)
    red, green, blue, left = state
    first, second = (encode(red, green), encode(blue, 1.0 - left))
    for s in range(count):
        out[s, 0] = first
        out[s, 1] = second


def frame_kernel(words, out):
    count, _, rows, cols = words.shape
    for s in range(count):
        here = slice(s * rows, (s + 1) * rows)
        for w in range(2):
            low, high = decode(words[s, w])
            out[2 * w, here, :] = low
            out[2 * w + 1, here, :] = high


def halo(array, axis, shift):
    count = lax.axis_size(axis)
    return lax.ppermute(array, axis, [(i, (i + shift) % count) for i in range(count)])


AXES = ("tx", "ty", "depth")


def neighbours():
    row = iota((8, 128), 0)
    flags = jnp.zeros((8, 128), jnp.float32)
    for i, axis in enumerate(AXES):
        place, count = (lax.axis_index(axis), lax.axis_size(axis))
        flags = jnp.where(row == 2 * i, (place > 0).astype(jnp.float32), flags)
        flags = jnp.where(row == 2 * i + 1, (place < count - 1).astype(jnp.float32), flags)
    return flags


def shards(volume, transfer, ray_start, ray_stop, pattern, depth_order):
    layers, rows, cols = volume.shape
    count = lax.axis_size("depth")
    bf16, f32 = (jnp.bfloat16, jnp.float32)
    limit = pltpu.CompilerParams(vmem_limit_bytes=20 * 1024 * 1024)
    vmem = pl.BlockSpec(memory_space=VMEM)
    smem = pl.BlockSpec(memory_space=SMEM)
    shape = jax.ShapeDtypeStruct

    hbm = pl.BlockSpec(memory_space=pltpu.HBM)
    anywhere = pl.BlockSpec(memory_space=pl.ANY)

    whole = shape((rows, cols), bf16)
    bounds = shape((rows, cols), jnp.int32)
    z0, z1, xt, field, begin, end, near = pl.pallas_call(
        open_kernel,
        out_shape=[whole] * 3 + [shape((layers, rows + 16, cols), f32)] + [bounds] * 2 + [shape((8, 128), f32)],
        in_specs=[hbm] * 3,
        out_specs=[vmem] * 7,
        scratch_shapes=[VMEM(volume.shape, bf16), pltpu.SemaphoreType.DMA((PARTS + 2,))],
        compiler_params=limit,
        name="open",
    )(*[pltpu.with_memory_space_constraint(x, pltpu.HBM) for x in (volume, ray_start[0], ray_stop[0])])
    zlo, zhi = (halo(z1, "depth", 1), halo(z0, "depth", -1))
    xlo, xhi = (halo(xt, "tx", 1), halo(xt, "tx", -1))
    y0, y1 = pl.pallas_call(
        rows_kernel,
        out_shape=[shape((layers, cols), bf16)] * 2,
        in_specs=[vmem, anywhere],
        out_specs=[vmem] * 2,
        compiler_params=limit,
        name="rows",
    )(field, zlo)
    ylo, yhi = (halo(y1, "ty", 1), halo(y0, "ty", -1))

    step_rows = 32
    share = rows // count
    slopes = transfer.T
    weights, alpha = pl.pallas_call(
        lambda *refs: absorb_kernel(*refs, count=count, step_rows=step_rows),
        out_shape=[shape((layers, rows, cols), f32), shape((rows, cols), f32)],
        in_specs=[smem, smem] + [vmem] * 3,
        out_specs=[vmem] * 2,
        compiler_params=limit,
        cost_estimate=pl.CostEstimate(
            flops=12 * volume.size, bytes_accessed=8 * volume.size, transcendentals=3 * volume.size
        ),
        name="absorb",
    )(slopes, pattern.reshape(-1), field, begin, end)
    words, _ = pl.pallas_call(
        lambda *refs: shade_kernel(*refs, count=count, step_rows=step_rows),
        out_shape=[shape((count, 2, share, cols), jnp.int32), shape(field.shape, f32)],
        in_specs=[smem] + [vmem] * 10,
        out_specs=[vmem] * 2,
        scratch_shapes=[VMEM((layers, step_rows, cols), f32)],
        input_output_aliases={1: 1},
        compiler_params=limit,
        cost_estimate=pl.CostEstimate(
            flops=40 * volume.size, bytes_accessed=8 * volume.size, transcendentals=4 * volume.size
        ),
        name="shade",
    )(slopes, field, weights, alpha, near, zlo, zhi, ylo, yhi, xlo, xhi)

    words = lax.all_to_all(words, "depth", split_axis=0, concat_axis=0, tiled=True)
    words = pl.pallas_call(
        composite_kernel,
        out_shape=shape(words.shape, jnp.int32),
        in_specs=[smem, vmem],
        out_specs=vmem,
        compiler_params=limit,
        name="composite",
    )(depth_order, words)
    words = lax.all_to_all(words, "depth", split_axis=0, concat_axis=0, tiled=True)
    return pl.pallas_call(
        frame_kernel,
        out_shape=shape((4, rows, cols), f32),
        in_specs=[vmem],
        out_specs=vmem,
        compiler_params=limit,
        name="frame",
    )(words)


def solution(mesh):
    in_specs = (
        P("depth", "ty", "tx"),
        P(),
        P("depth", "ty", "tx"),
        P("depth", "ty", "tx"),
        P("depth", "ty", "tx"),
        P(),
    )
    out_specs = P(None, "ty", "tx")
    return jax.shard_map(shards, mesh=mesh, in_specs=in_specs, out_specs=out_specs, check_vma=False)
```

```python
import jax
import jax.numpy as jnp
from jax import lax
from jax.experimental import pallas as pl
from jax.experimental.pallas import tpu as pltpu
from jax.sharding import PartitionSpec as P

LOG2E = 1.4426950408889634
CODE = 65535.0
PARTS = 2
VMEM = pltpu.VMEM
SMEM = pltpu.SMEM


def iota(shape, dim):
    return lax.broadcasted_iota(jnp.int32, shape, dim)


def encode(low, high):
    def code(x):
        root = jnp.sqrt(jnp.sqrt(jnp.maximum(x, 0.0)))
        return jnp.minimum(root * CODE + 0.5, CODE).astype(jnp.int32)

    return code(low) | (code(high) << 16)


def decode(word):
    def value(c):
        square = (c.astype(jnp.float32) * (1.0 / CODE)) ** 2
        return square * square

    return value(word & 0xFFFF), value(lax.shift_right_logical(word, 16))


def open_kernel(volume, start, stop, z0, z1, xt, field, begin, end, near, vol, sems):
    layers, rows, cols = vol.shape
    parts = sems.shape[0] - 2
    each = layers // parts
    copies = [
        pltpu.make_async_copy(
            volume.at[pl.ds(p * each, each)], vol.at[pl.ds(p * each, each)], sems.at[p]
        )
        for p in range(parts)
    ]
    copies.append(pltpu.make_async_copy(start, begin, sems.at[parts]))
    copies.append(pltpu.make_async_copy(stop, end, sems.at[parts + 1]))
    for copy in copies:
        copy.start()
    near[...] = neighbours()
    r, c = (iota((2 * cols, cols), 0), iota((2 * cols, cols), 1))
    column, second = (r % cols, r // cols)
    total = jnp.zeros((rows, cols), jnp.float32)
    for k in range(0, layers, 2):
        if k % each == 0:
            copies[k // each].wait()
        lane = 2 * (k + second)
        pick = ((column == 0) & (c == lane)) | ((column == cols - 1) & (c == (lane + cols - 1) % cols))
        one, two = (vol[k], vol[k + 1])
        field[k, 8 : rows + 8, :] = one.astype(jnp.float32)
        field[k + 1, 8 : rows + 8, :] = two.astype(jnp.float32)
        total = total + jnp.dot(
            jnp.concatenate([one, two], axis=1),
            pick.astype(jnp.float32).astype(jnp.bfloat16),
            preferred_element_type=jnp.float32,
        )
    z0[...] = vol[0]
    z1[...] = vol[layers - 1]
    xt[...] = total.astype(jnp.bfloat16)
    for copy in copies[parts:]:
        copy.wait()


def rows_kernel(field, arrived, y0, y1):
    rows = field.shape[1] - 16
    y0[...] = field[:, 8:16, :][:, 0, :].astype(jnp.bfloat16)
    y1[...] = field[:, rows : rows + 8, :][:, 7, :].astype(jnp.bfloat16)


def absorb_kernel(tf, pat, field, begin, end, weights, alpha, *, count, step_rows):
    layers, rows, cols = weights.shape
    f32 = jnp.float32
    slope, offset = (tf[0, 3] * LOG2E, tf[1, 3] * LOG2E)
    scale = -LOG2E * 2.0 / (layers * count)
    half = layers // 2

    def chunk(i, carry):
        base = pl.multiple_of(i * step_rows, step_rows)
        here = pl.ds(base, step_rows)
        middle = pl.ds(pl.multiple_of(base + 8, 8), step_rows)
        group = iota((step_rows, cols), 0) // 8
        on = jnp.zeros((step_rows, cols), jnp.int32)
        for g in range(step_rows // 8):
            on = jnp.where(group == g, pat[i * (step_rows // 8) + g], on)
        enter = jnp.where(on > 0, begin[here, :], layers)
        leave = jnp.where(on > 0, end[here, :], 0)
        depth = jnp.zeros((step_rows, cols), f32)
        before = depth + 1.0
        for k in range(layers):
            soft = jnp.log(1.0 + jnp.exp2(slope * field[k, middle, :] + offset))
            active = enter <= k if k < half else leave > k
            depth = depth + jnp.where(active, soft, 0.0)
            after = jnp.exp2(depth * scale)
            weights[k, here, :] = before - after
            before = after
        alpha[here, :] = 1.0 - before
        return carry

    lax.fori_loop(0, rows // step_rows, chunk, 0)


def shade_kernel(
    tf, middle_rows, weights, alpha, near, zlo, zhi, ylo, yhi, xlo, xhi, out, field, ends,
    sides, first_layer, last_layer, *, count, step_rows
):
    del middle_rows
    layers, rows, cols = weights.shape
    f32 = jnp.float32
    sub = iota((layers, 8, cols), 1)
    kept = [(near[2 * i : 2 * i + 1, :], near[2 * i + 1 : 2 * i + 2, :]) for i in range(len(AXES))]
    low, high = kept[0]
    even = iota((rows, cols), 1) % 2 == 0
    sides[...] = jnp.where(even, xhi[...].astype(f32) * high, xlo[...].astype(f32) * low)
    low, high = kept[2]
    first_layer[...] = zlo[...].astype(f32) * low
    last_layer[...] = zhi[...].astype(f32) * high
    low, high = kept[1]
    field[:, 0:8, :] = jnp.where(sub == 7, (ylo[...].astype(f32) * low)[:, None, :], 0.0)
    field[:, rows + 8 : rows + 16, :] = jnp.where(
        sub == 0, (yhi[...].astype(f32) * high)[:, None, :], 0.0
    )

    slopes = [tf[0, j] * 0.5 for j in range(3)]
    offsets = [tf[1, j] * 0.5 for j in range(3)]
    strength = 0.64 * 0.7
    lane = iota((step_rows, cols), 1)
    first_lane, last_lane = (lane == 0, lane == cols - 1)

    def chunk(i, carry):
        base = pl.multiple_of(i * step_rows, step_rows)
        here = pl.ds(base, step_rows)
        middle = pl.ds(pl.multiple_of(base + 8, 8), step_rows)
        around = sides[here, :]
        for k in range(layers):
            ends[k] = around if k == 0 else pltpu.roll(around, cols - 2 * k, 1)
        zero = jnp.zeros((step_rows, cols), f32)
        shaded, tints = (zero, [zero, zero, zero])
        below, value = (first_layer[here, :], field[0, middle, :])
        for k in range(layers):
            above = field[k + 1, middle, :] if k + 1 < layers else last_layer[here, :]
            right = pltpu.roll(jnp.where(first_lane, ends[k], value), cols - 1, 1)
            left = pltpu.roll(jnp.where(last_lane, ends[k], value), 1, 1)
            sx, sz = (right - left, above - below)
            sy = field[k, pl.ds(base + 9, step_rows), :] - field[k, pl.ds(base + 7, step_rows), :]
            lit = jnp.abs((0.48 / 0.64) * sx + (0.6 / 0.64) * sy + sz)
            bright = lit * lax.rsqrt(sx * sx + sy * sy + sz * sz + 4.0) + 0.3 / strength
            weight = weights[k, here, :] * bright
            shaded = shaded + weight
            tints = [
                t + weight * jnp.tanh(s * value + o) for t, s, o in zip(tints, slopes, offsets)
            ]
            below, value = (value, above)
        red, green, blue = [(0.5 * strength) * (shaded + t) for t in tints]
        first, second = (encode(red, green), encode(blue, alpha[here, :]))
        share = rows // count
        for j in range(step_rows // share):
            out[i * (step_rows // share) + j, 0] = first[j * share : (j + 1) * share]
            out[i * (step_rows // share) + j, 1] = second[j * share : (j + 1) * share]
        return carry

    lax.fori_loop(0, rows // step_rows, chunk, 0)


def composite_kernel(order, parts, out):
    count, _, rows, cols = parts.shape

    def step(r, state):
        red, green, blue, left = state
        s = order[r]
        one, two = (decode(parts[s, 0]), decode(parts[s, 1]))
        return (red + left * one[0], green + left * one[1], blue + left * two[0], left * (1.0 - two[1]))

    zero = jnp.zeros((rows, cols), jnp.float32)
    state = (zero, zero, zero, zero + 1.0)
    for r in range(count):
        state = step(r, state)
    red, green, blue, left = state
    first, second = (encode(red, green), encode(blue, 1.0 - left))
    for s in range(count):
        out[s, 0] = first
        out[s, 1] = second


def frame_kernel(words, out):
    count, _, rows, cols = words.shape
    for s in range(count):
        here = slice(s * rows, (s + 1) * rows)
        for w in range(2):
            low, high = decode(words[s, w])
            out[2 * w, here, :] = low
            out[2 * w + 1, here, :] = high


def halo(array, axis, shift):
    count = lax.axis_size(axis)
    return lax.ppermute(array, axis, [(i, (i + shift) % count) for i in range(count)])


AXES = ("tx", "ty", "depth")


def neighbours():
    row = iota((8, 128), 0)
    flags = jnp.zeros((8, 128), jnp.float32)
    for i, axis in enumerate(AXES):
        place, count = (lax.axis_index(axis), lax.axis_size(axis))
        flags = jnp.where(row == 2 * i, (place > 0).astype(jnp.float32), flags)
        flags = jnp.where(row == 2 * i + 1, (place < count - 1).astype(jnp.float32), flags)
    return flags


def shards(volume, transfer, ray_start, ray_stop, pattern, depth_order):
    layers, rows, cols = volume.shape
    count = lax.axis_size("depth")
    bf16, f32 = (jnp.bfloat16, jnp.float32)
    limit = pltpu.CompilerParams(vmem_limit_bytes=20 * 1024 * 1024)
    vmem = pl.BlockSpec(memory_space=VMEM)
    smem = pl.BlockSpec(memory_space=SMEM)
    shape = jax.ShapeDtypeStruct

    hbm = pl.BlockSpec(memory_space=pltpu.HBM)
    anywhere = pl.BlockSpec(memory_space=pl.ANY)

    whole = shape((rows, cols), bf16)
    bounds = shape((rows, cols), jnp.int32)
    z0, z1, xt, field, begin, end, near = pl.pallas_call(
        open_kernel,
        out_shape=[whole] * 3 + [shape((layers, rows + 16, cols), f32)] + [bounds] * 2 + [shape((8, 128), f32)],
        in_specs=[hbm] * 3,
        out_specs=[vmem] * 7,
        scratch_shapes=[VMEM(volume.shape, bf16), pltpu.SemaphoreType.DMA((PARTS + 2,))],
        compiler_params=limit,
        name="open",
    )(*[pltpu.with_memory_space_constraint(x, pltpu.HBM) for x in (volume, ray_start[0], ray_stop[0])])
    zlo, zhi = (halo(z1, "depth", 1), halo(z0, "depth", -1))
    xlo, xhi = (halo(xt, "tx", 1), halo(xt, "tx", -1))
    y0, y1 = pl.pallas_call(
        rows_kernel,
        out_shape=[shape((layers, cols), bf16)] * 2,
        in_specs=[vmem, anywhere],
        out_specs=[vmem] * 2,
        compiler_params=limit,
        name="rows",
    )(field, zlo)
    ylo, yhi = (halo(y1, "ty", 1), halo(y0, "ty", -1))

    step_rows = 32
    share = rows // count
    slopes = transfer.T
    weights, alpha = pl.pallas_call(
        lambda *refs: absorb_kernel(*refs, count=count, step_rows=step_rows),
        out_shape=[shape((layers, rows, cols), f32), shape((rows, cols), f32)],
        in_specs=[smem, smem] + [vmem] * 3,
        out_specs=[vmem] * 2,
        compiler_params=limit,
        cost_estimate=pl.CostEstimate(
            flops=12 * volume.size, bytes_accessed=8 * volume.size, transcendentals=3 * volume.size
        ),
        name="absorb",
    )(slopes, pattern.reshape(-1), field, begin, end)
    words, _ = pl.pallas_call(
        lambda *refs: shade_kernel(*refs, count=count, step_rows=step_rows),
        out_shape=[shape((count, 2, share, cols), jnp.int32), shape(field.shape, f32)],
        in_specs=[smem] + [vmem] * 10,
        out_specs=[vmem] * 2,
        scratch_shapes=[VMEM((layers, step_rows, cols), f32)] + [VMEM((rows, cols), f32)] * 3,
        input_output_aliases={1: 1},
        compiler_params=limit,
        cost_estimate=pl.CostEstimate(
            flops=40 * volume.size, bytes_accessed=8 * volume.size, transcendentals=4 * volume.size
        ),
        name="shade",
    )(slopes, field, weights, alpha, near, zlo, zhi, ylo, yhi, xlo, xhi)

    words = lax.all_to_all(words, "depth", split_axis=0, concat_axis=0, tiled=True)
    words = pl.pallas_call(
        composite_kernel,
        out_shape=shape(words.shape, jnp.int32),
        in_specs=[smem, vmem],
        out_specs=vmem,
        compiler_params=limit,
        name="composite",
    )(depth_order, words)
    words = lax.all_to_all(words, "depth", split_axis=0, concat_axis=0, tiled=True)
    return pl.pallas_call(
        frame_kernel,
        out_shape=shape((4, rows, cols), f32),
        in_specs=[vmem],
        out_specs=vmem,
        compiler_params=limit,
        name="frame",
    )(words)


def solution(mesh):
    in_specs = (
        P("depth", "ty", "tx"),
        P(),
        P("depth", "ty", "tx"),
        P("depth", "ty", "tx"),
        P("depth", "ty", "tx"),
        P(),
    )
    out_specs = P(None, "ty", "tx")
    return jax.shard_map(shards, mesh=mesh, in_specs=in_specs, out_specs=out_specs, check_vma=False)
```
